32 devices in a mesh: dp: 8 (over z, core), ctx: 4 (over y, x).
Axes of the slice: x: 2, y: 2, z: 4, core: 2. Of those that a mesh axis runs over, the one named last changes fastest.
Arguments:
- query_rows: bfloat16 [1536, 8, 640], P(('dp', 'ctx')), parts along dimension 0, may hold values from -6 to 6
- key_rows: bfloat16 [1536, 8, 640], P(('dp', 'ctx')), parts along dimension 0, may hold values from -6 to 6
- value_rows: bfloat16 [1536, 8, 640], P(('dp', 'ctx')), parts along dimension 0, may hold values from -6 to 6
- token_rates: bfloat16 [1536, 8], P(('dp', 'ctx')), parts along dimension 0, may hold values from 0.099609375 to 1
- fast_weights: float32 [8, 3, 640, 1280], P('ctx'), may hold values from -0.25 to 0.25
Outputs:
- outputs: bfloat16 [1536, 8, 640], P(('dp', 'ctx')), parts along dimension 0
- new_weights: float32 [64, 3, 640, 1280], P(('dp', 'ctx')), parts along dimension 0
The draws below stay inside these ranges and needn't reach their ends.
There are 8 independent parts, one for each index of `dp`. The reference program is written for one: setup_inputs(seed, part) draws one part's arguments, and reference() takes and returns one part's arrays. A program takes and returns all parts, laid end to end along the dimension named above; an argument that names none is the same for every part. Nothing has to cross between parts.
All inputs are finite; a program needn't handle non-finite values.
Results may differ from the reference program's by a relative error of at most 0.019.
Values may be sent and summed in bfloat16 or wider, within the bound.
A program may use at most 192 MiB of HBM per device.

```python
import math
import jax
import jax.numpy as jnp
from jax import lax

HEADS = 8
DH = 640
HID = 1280
NS_ITERS = 3
TOKENS = 192
N_CTX = 4


def shard_levels(rng, extent, pieces, low, top_value):
    def one(axis_at, shards_of):
        draws = jax.random.uniform(jax.random.fold_in(jax.random.fold_in(rng, 6), axis_at), (shards_of,), jnp.float32, low / len(pieces), top_value / len(pieces))
        return jnp.repeat(jnp.exp(draws), extent[axis_at] // shards_of).reshape((-1,) + (1,) * (len(extent) - axis_at - 1))

    loudness = one(*pieces[0])
    for cut in pieces[1:]:
        loudness = loudness * one(*cut)
    return loudness


def normal_values(rng, shape, width, limit, cuts=(), dtype=jnp.bfloat16):
    level = shard_levels(rng, shape, cuts, -0.22, 0.18) if cuts else 1.0
    values = jax.random.normal(rng, shape, jnp.float32) * width * level
    return jnp.minimum(jnp.maximum(values, -limit), limit).astype(dtype)


def setup_inputs(seed: int = 0, part: int = 0) -> dict:
    streams_of = jax.random.split(jax.random.key(seed), 6)
    part_splits = jax.random.split(jax.random.fold_in(streams_of[5], part), 6)
    query_rows = normal_values(part_splits[0], (TOKENS, HEADS, DH), 1.0, 6.0, ((0, 4),))
    key_rows = normal_values(part_splits[1], (TOKENS, HEADS, DH), 1.0, 6.0, ((0, 4),))
    value_rows = normal_values(part_splits[2], (TOKENS, HEADS, DH), 1.0, 6.0, ((0, 4),))
    token_rates = jnp.clip(jnp.exp(math.log(1.0) - 2.306499 * jax.random.uniform(part_splits[3], (TOKENS, HEADS), jnp.float32) ** shard_levels(part_splits[3], (TOKENS, HEADS), ((0, 4),), -0.2, 0.2)), 0.099609375, 1.0).astype(jnp.bfloat16)
    fast_weights = normal_values(streams_of[4], (HEADS, 3, DH, HID), DH ** -0.5, 0.25, ((0, 4),), jnp.float32)
    return {"query_rows": query_rows, "key_rows": key_rows, "value_rows": value_rows, "token_rates": token_rates, "fast_weights": fast_weights}


linear_term = 3.4445
cubic_term = -4.775
quintic_term = 2.0315

def split_blocks(rows, block_count):
    return rows.reshape(block_count, rows.shape[0] // block_count, rows.shape[-1]).astype(jnp.float32)

def block_sum(left, right):
    partial_terms = jnp.einsum('ntd,nth->ndh', left, right).astype(jnp.bfloat16)
    partial_terms = lax.optimization_barrier(partial_terms)
    return lax.optimization_barrier(jnp.sum(partial_terms.astype(jnp.float32), axis=0))

def orthogonal(grad_matrix):
    ortho = (grad_matrix * lax.rsqrt(jnp.sum(grad_matrix * grad_matrix) + 1e-06)).astype(jnp.bfloat16)
    for _ in range(NS_ITERS):
        gram = jnp.dot(ortho, ortho.T, preferred_element_type=jnp.float32).astype(jnp.bfloat16)
        square = jnp.dot(gram, gram, preferred_element_type=jnp.float32)
        combined = (cubic_term * gram.astype(jnp.float32) + quintic_term * square).astype(jnp.bfloat16)
        mixed = jnp.dot(combined, ortho, preferred_element_type=jnp.float32)
        ortho = (linear_term * ortho.astype(jnp.float32) + mixed).astype(jnp.bfloat16)
    return ortho

def head_update(key_head, value_head, rate_head, weights_head):
    weights_bf = weights_head.astype(jnp.bfloat16)
    gate_pre = jnp.dot(key_head, weights_bf[0], preferred_element_type=jnp.float32)
    up_proj = jnp.dot(key_head, weights_bf[1], preferred_element_type=jnp.float32)
    sigmoid_gate = jax.nn.sigmoid(gate_pre)
    silu_gate = gate_pre * sigmoid_gate
    hidden = (silu_gate * up_proj).astype(jnp.bfloat16)
    scaled = (rate_head.astype(jnp.float32)[:, None] * value_head.astype(jnp.float32)).astype(jnp.bfloat16)
    back_grad = -jnp.dot(scaled, weights_bf[2], preferred_element_type=jnp.float32)
    grad_gate = (back_grad * up_proj * sigmoid_gate * (1.0 + gate_pre * (1.0 - sigmoid_gate))).astype(jnp.bfloat16)
    grad_up = (back_grad * silu_gate).astype(jnp.bfloat16)
    key_blocks = split_blocks(key_head, N_CTX)
    first = block_sum(key_blocks, split_blocks(grad_gate, N_CTX))
    second = block_sum(key_blocks, split_blocks(grad_up, N_CTX))
    third = -block_sum(split_blocks(scaled, N_CTX), split_blocks(hidden, N_CTX))
    step_scale = math.sqrt(DH / HID)
    updated = []
    for index, grad_matrix in enumerate([first, second, third]):
        updated.append(weights_head[index] - step_scale * orthogonal(grad_matrix).astype(jnp.float32))
    return jnp.stack(updated)

def apply_head(query_head, weights_bf):
    gate_pre = jnp.dot(query_head, weights_bf[0], preferred_element_type=jnp.float32)
    up_proj = jnp.dot(query_head, weights_bf[1], preferred_element_type=jnp.float32)
    hidden = (jax.nn.silu(gate_pre) * up_proj).astype(jnp.bfloat16)
    result = lax.dot_general(hidden, weights_bf[2], (((1,), (1,)), ((), ())), preferred_element_type=jnp.float32)
    return result.astype(jnp.bfloat16)

def reference(query_rows, key_rows, value_rows, token_rates, fast_weights):
    new_weights = lax.map(lambda items: head_update(*items), (jnp.transpose(key_rows, (1, 0, 2)), jnp.transpose(value_rows, (1, 0, 2)), jnp.transpose(token_rates, (1, 0)), fast_weights))
    applied = new_weights.astype(jnp.bfloat16)
    results = lax.map(lambda items: apply_head(*items), (jnp.transpose(query_rows, (1, 0, 2)), applied))
    return (jnp.transpose(results, (1, 0, 2)), new_weights)
```

```python
import math

import jax
import jax.numpy as jnp
from jax import lax
from jax.sharding import PartitionSpec as P

NS_ITERS = 3

linear_term = 3.4445
cubic_term = -4.775
quintic_term = 2.0315


def mm(left, right):
    return jnp.einsum(
        "...ij,...jk->...ik",
        left,
        right,
        precision=lax.Precision.HIGHEST,
        preferred_element_type=jnp.float32,
    )


def gram(rows):
    return jnp.einsum("...ih,...jh->...ij", rows, rows, preferred_element_type=jnp.float32)


def factor_chain(square, key_gram):
    norm = jnp.maximum(jnp.sum(square * key_gram, axis=(-2, -1), keepdims=True), 0.0)
    inverse = lax.rsqrt(norm + 1e-06)
    power = mm(square * (inverse * inverse), key_gram)
    eye = jnp.eye(square.shape[-1], dtype=jnp.float32)
    total = None
    for step in range(NS_ITERS):
        squared = mm(power, power)
        poly = linear_term * eye + cubic_term * power + quintic_term * squared
        total = poly if total is None else mm(poly, total)
        if step < NS_ITERS - 1:
            power = mm(poly, mm(poly, power))
    return total * inverse


def body(query_rows, key_rows, value_rows, token_rates, fast_weights):
    ctx_count = lax.axis_size("ctx")
    local = fast_weights.shape[0]
    tokens, heads, width = key_rows.shape
    scaled = (
        token_rates.astype(jnp.float32)[:, :, None] * value_rows.astype(jnp.float32)
    ).astype(jnp.bfloat16)
    packed = jnp.stack([key_rows, scaled, query_rows]).transpose(2, 0, 1, 3)
    moved = lax.all_to_all(packed, "ctx", split_axis=0, concat_axis=0, tiled=True)
    moved = moved.reshape(ctx_count, local, 3, tokens, width).transpose(1, 2, 0, 3, 4)
    moved = moved.reshape(local, 3, ctx_count * tokens, width)
    keys, scaled, queries = moved[:, 0], moved[:, 1], moved[:, 2]

    weights_bf = fast_weights.astype(jnp.bfloat16)
    dot = lambda a, b: jnp.einsum("ltd,ldh->lth", a, b, preferred_element_type=jnp.float32)
    gate_pre = dot(keys, weights_bf[:, 0])
    up_proj = dot(keys, weights_bf[:, 1])
    back_grad = -dot(scaled, weights_bf[:, 2])
    sigmoid_gate = jax.nn.sigmoid(gate_pre)
    silu_gate = gate_pre * sigmoid_gate
    hidden = (silu_gate * up_proj).astype(jnp.bfloat16)
    grad_gate = (
        back_grad * up_proj * sigmoid_gate * (1.0 + gate_pre * (1.0 - sigmoid_gate))
    ).astype(jnp.bfloat16)
    grad_up = (back_grad * silu_gate).astype(jnp.bfloat16)
    rights = jnp.stack([grad_gate, grad_up, hidden], axis=1)
    key_gram, scaled_gram = gram(keys), gram(scaled)
    lefts_gram = jnp.stack([key_gram, key_gram, scaled_gram], axis=1)
    chain = factor_chain(gram(rights), lefts_gram).astype(jnp.bfloat16)
    mixed = jnp.einsum("lkij,lkjh->lkih", chain, rights, preferred_element_type=jnp.float32)
    mixed = mixed.astype(jnp.bfloat16)
    lefts = jnp.stack([keys, keys, -scaled], axis=1)
    ortho = jnp.einsum("lktd,lkth->lkdh", lefts, mixed, preferred_element_type=jnp.float32)
    step_scale = math.sqrt(fast_weights.shape[-2] / fast_weights.shape[-1])
    new_weights = fast_weights - step_scale * ortho
    applied = new_weights.astype(jnp.bfloat16)

    hidden = (
        jax.nn.silu(dot(queries, applied[:, 0])) * dot(queries, applied[:, 1])
    ).astype(jnp.bfloat16)
    result = jnp.einsum(
        "lth,ldh->ltd", hidden, applied[:, 2], preferred_element_type=jnp.float32
    ).astype(jnp.bfloat16)
    result = result.reshape(local, ctx_count, tokens, width).transpose(1, 0, 2, 3)
    result = result.reshape(heads, tokens, width)
    outputs = lax.all_to_all(result, "ctx", split_axis=0, concat_axis=0, tiled=True)
    return (outputs.transpose(1, 0, 2), new_weights)


def solution(mesh):
    placed = (
        P(("dp", "ctx"), None, None),
        P(("dp", "ctx"), None, None),
        P(("dp", "ctx"), None, None),
        P(("dp", "ctx"), None),
        P("ctx", None, None, None),
    )
    return jax.shard_map(
        body,
        mesh=mesh,
        in_specs=placed,
        out_specs=(P(("dp", "ctx"), None, None), P(("dp", "ctx"), None, None, None)),
        check_vma=False,
    )
```

```python
import functools
import math

import jax
import jax.numpy as jnp
from jax import lax
from jax.experimental import pallas as pl
from jax.experimental.pallas import tpu as pltpu
from jax.sharding import PartitionSpec as P

NS_ITERS = 3
TILE = 256
MESH = pl.DeviceIdType.MESH

linear_term = 3.4445
cubic_term = -4.775
quintic_term = 2.0315


def dot(left, right):
    return jnp.dot(left, right, preferred_element_type=jnp.float32)


def dot_rows(left, right):
    return lax.dot_general(
        left, right, (((1,), (1,)), ((), ())), preferred_element_type=jnp.float32
    )


def split(values):
    high = values.astype(jnp.bfloat16)
    return high, (values - high.astype(jnp.float32)).astype(jnp.bfloat16)


def mm(left, right):
    return dot(left[0], right[0]) + (dot(left[0], right[1]) + dot(left[1], right[0]))


def factor_chain(squares, key_grams, scales):
    size = squares[0].shape[0]
    row = lax.broadcasted_iota(jnp.int32, (size, size), 0)
    col = lax.broadcasted_iota(jnp.int32, (size, size), 1)
    eye = jnp.where(row == col, jnp.float32(linear_term), jnp.float32(0.0))
    inverses, powers = [], []
    for square, key_gram in zip(squares, key_grams):
        norm = jnp.maximum(jnp.sum(square * key_gram, keepdims=True), 0.0)
        inverses.append(lax.rsqrt(norm + 1e-06))
    key_splits = {id(g): split(g) for g in key_grams}
    for square, key_gram, inverse in zip(squares, key_grams, inverses):
        powers.append(mm(split(square * (inverse * inverse)), key_splits[id(key_gram)]))
    totals = None
    for step in range(NS_ITERS):
        parts = [split(p) for p in powers]
        squared = [mm(p, p) for p in parts]
        polys = [
            split(eye + cubic_term * p + quintic_term * s) for p, s in zip(powers, squared)
        ]
        if step < NS_ITERS - 1:
            once = [split(mm(q, p)) for q, p in zip(polys, parts)]
            powers = [mm(q, o) for q, o in zip(polys, once)]
        if totals is None:
            totals = polys
        elif step < NS_ITERS - 1:
            totals = [split(mm(q, t)) for q, t in zip(polys, totals)]
        else:
            totals = [mm(q, t) for q, t in zip(polys, totals)]
    return [t * (i * s) for t, i, s in zip(totals, inverses, scales)]


def owner_kernel(
    n, packed, weights, mixed, lefts, result,
    moved, held, rights, chain, total, send_sem, recv_sem, own_sem, weight_sem,
):
    local, width, hid = held.shape[0], held.shape[2], held.shape[3]
    tokens = n * moved.shape[3]
    me = lax.axis_index("ctx")

    loads = {}
    for l in range(local):
        for k in range(3):
            loads[l, k] = pltpu.make_async_copy(
                weights.at[l, k], held.at[l, k], weight_sem.at[l, k]
            )

    barrier = pltpu.get_barrier_semaphore()
    for j in range(1, n):
        pl.semaphore_signal(
            barrier, inc=1, device_id={"ctx": lax.rem(me + j, n)}, device_id_type=MESH
        )
    pl.semaphore_wait(barrier, n - 1)

    groups = (pl.ds(0, 2), pl.ds(2, 1))
    sends, owns = {}, {}
    for g in range(2):
        for l in range(local):
            owns[l, g] = pltpu.make_async_copy(
                packed.at[me, l, groups[g]], moved.at[me, l, groups[g]], own_sem.at[l, g]
            )
            owns[l, g].start()
            for j in range(1, n):
                target = lax.rem(me + j, n)
                sends[j, l, g] = pltpu.make_async_remote_copy(
                    src_ref=packed.at[target, l, groups[g]],
                    dst_ref=moved.at[me, l, groups[g]],
                    send_sem=send_sem.at[j - 1, l, g],
                    recv_sem=recv_sem.at[j - 1, l, g],
                    device_id={"ctx": target},
                    device_id_type=MESH,
                )
                sends[j, l, g].start()
    for l in range(local):
        for k in range(3):
            loads[l, k].start()

    def arrived(l, g):
        owns[l, g].wait()
        for j in range(1, n):
            sends[j, l, g].wait_recv()

    def rows(l, k):
        return moved[:, l, k].reshape(tokens, width)

    def columns(j):
        return pl.ds(pl.multiple_of(j * TILE, TILE), TILE)

    for l in range(local):
        arrived(l, 0)
        for k in range(3):
            loads[l, k].wait()

        @pl.loop(0, hid // TILE)
        def _(j):
            cols = columns(j)
            keys, scaled = rows(l, 0), rows(l, 1)
            gate_pre = dot(keys, held[l, 0, :, cols].astype(jnp.bfloat16))
            up_proj = dot(keys, held[l, 1, :, cols].astype(jnp.bfloat16))
            back_grad = -dot(scaled, held[l, 2, :, cols].astype(jnp.bfloat16))
            sigmoid_gate = jax.nn.sigmoid(gate_pre)
            silu_gate = gate_pre * sigmoid_gate
            rights[l, 0, :, cols] = (
                back_grad * up_proj * sigmoid_gate * (1.0 + gate_pre * (1.0 - sigmoid_gate))
            ).astype(jnp.bfloat16)
            rights[l, 1, :, cols] = (back_grad * silu_gate).astype(jnp.bfloat16)
            rights[l, 2, :, cols] = (silu_gate * up_proj).astype(jnp.bfloat16)

    step_scale = math.sqrt(width / hid)

    @pl.loop(0, local)
    def _(l):
        keys, scaled = rows(l, 0), rows(l, 1)
        lefts[l, 0] = keys.T
        lefts[l, 1] = scaled.T
        key_gram, scaled_gram = dot_rows(keys, keys), dot_rows(scaled, scaled)
        squares = [dot_rows(rights[l, k], rights[l, k]) for k in range(3)]
        factors = factor_chain(
            squares,
            [key_gram, key_gram, scaled_gram],
            [-step_scale, -step_scale, step_scale],
        )
        for k in range(3):
            chain[l, k] = factors[k].astype(jnp.bfloat16)

        @pl.loop(0, hid // TILE)
        def _(j):
            cols = columns(j)
            for k in range(3):
                mixed[l, k, :, cols] = dot(chain[l, k], rights[l, k, :, cols]).astype(
                    jnp.bfloat16
                )

    for l in range(local):
        arrived(l, 1)
        total[...] = jnp.zeros_like(total)

        @pl.loop(0, hid // TILE)
        def _(j):
            cols = columns(j)
            queries = rows(l, 2)
            applied = [
                (held[l, k, :, cols] + dot(lefts[l, k // 2], mixed[l, k, :, cols])).astype(
                    jnp.bfloat16
                )
                for k in range(3)
            ]
            gate_pre, up_proj = dot(queries, applied[0]), dot(queries, applied[1])
            hidden = (gate_pre * jax.nn.sigmoid(gate_pre) * up_proj).astype(jnp.bfloat16)
            total[...] += dot_rows(hidden, applied[2])

        result[:, l] = total[...].astype(jnp.bfloat16).reshape(result[:, l].shape)

    for copy in sends.values():
        copy.wait_send()


def owner_step(packed, fast_weights, n):
    local, _, width, hid = fast_weights.shape
    tokens = n * packed.shape[3]
    bf16, vmem = jnp.bfloat16, pl.BlockSpec(memory_space=pltpu.VMEM)
    return pl.pallas_call(
        functools.partial(owner_kernel, n),
        out_shape=(
            jax.ShapeDtypeStruct((local, 3, tokens, hid), bf16),
            jax.ShapeDtypeStruct((local, 2, width, tokens), bf16),
            jax.ShapeDtypeStruct((n, local, packed.shape[3], width), bf16),
        ),
        in_specs=[pl.BlockSpec(memory_space=pl.ANY)] * 2,
        out_specs=(vmem, vmem, vmem),
        scratch_shapes=[
            pltpu.VMEM(packed.shape, bf16),
            pltpu.VMEM(fast_weights.shape, jnp.float32),
            pltpu.VMEM((local, 3, tokens, hid), bf16),
            pltpu.VMEM((local, 3, tokens, tokens), bf16),
            pltpu.VMEM((tokens, width), jnp.float32),
            pltpu.SemaphoreType.DMA((n - 1, local, 2)),
            pltpu.SemaphoreType.DMA((n - 1, local, 2)),
            pltpu.SemaphoreType.DMA((local, 2)),
            pltpu.SemaphoreType.DMA((local, 3)),
        ],
        compiler_params=pltpu.CompilerParams(
            collective_id=0, has_side_effects=True, vmem_limit_bytes=48 * 2**20
        ),
    )(packed, fast_weights)


def update_kernel(weights, lefts, mixed, out):
    out[0, 0] = weights[0, 0] + dot(lefts[0, 0], mixed[0, 0])


def update(fast_weights, lefts, mixed):
    local, kinds, width, hid = fast_weights.shape
    tokens, half = mixed.shape[2], hid // 2
    block = pl.BlockSpec((1, 1, width, half), lambda l, k, j: (l, k, 0, j))
    return pl.pallas_call(
        update_kernel,
        grid=(local, kinds, 2),
        out_shape=jax.ShapeDtypeStruct(fast_weights.shape, jnp.float32),
        in_specs=[
            block,
            pl.BlockSpec((1, 1, width, tokens), lambda l, k, j: (l, k // 2, 0, 0)),
            pl.BlockSpec((1, 1, tokens, half), lambda l, k, j: (l, k, 0, j)),
        ],
        out_specs=block,
        compiler_params=pltpu.CompilerParams(vmem_limit_bytes=32 * 2**20),
        cost_estimate=pl.CostEstimate(
            flops=2 * fast_weights.size * tokens,
            bytes_accessed=8 * fast_weights.size + 2 * (lefts.size + mixed.size),
            transcendentals=0,
        ),
    )(fast_weights, lefts, mixed)


def body(query_rows, key_rows, value_rows, token_rates, fast_weights):
    n = lax.axis_size("ctx")
    local = fast_weights.shape[0]
    tokens, heads, width = key_rows.shape
    scaled = (
        token_rates.astype(jnp.float32)[:, :, None] * value_rows.astype(jnp.float32)
    ).astype(jnp.bfloat16)
    packed = jnp.stack([key_rows, scaled, query_rows]).transpose(2, 0, 1, 3)
    packed = packed.reshape(n, local, 3, tokens, width)
    mixed, lefts, result = owner_step(packed, fast_weights, n)
    outputs = lax.all_to_all(
        result.reshape(heads, tokens, width), "ctx", split_axis=0, concat_axis=0, tiled=True
    )
    new_weights = update(fast_weights, lefts, mixed)
    return (outputs.transpose(1, 0, 2), new_weights)


def solution(mesh):
    placed = (
        P(("dp", "ctx"), None, None),
        P(("dp", "ctx"), None, None),
        P(("dp", "ctx"), None, None),
        P(("dp", "ctx"), None),
        P("ctx", None, None, None),
    )
    return jax.shard_map(
        body,
        mesh=mesh,
        in_specs=placed,
        out_specs=(P(("dp", "ctx"), None, None), P(("dp", "ctx"), None, None, None)),
        check_vma=False,
    )
```

```python
import functools
import math

import jax
import jax.numpy as jnp
from jax import lax
from jax.experimental import pallas as pl
from jax.experimental.pallas import tpu as pltpu
from jax.sharding import PartitionSpec as P

NS_ITERS = 3
TILE = 256
MESH = pl.DeviceIdType.MESH

linear_term = 3.4445
cubic_term = -4.775
quintic_term = 2.0315


def dot(left, right):
    return jnp.dot(left, right, preferred_element_type=jnp.float32)


def dot_rows(left, right):
    return lax.dot_general(
        left, right, (((1,), (1,)), ((), ())), preferred_element_type=jnp.float32
    )


def split(values):
    high = values.astype(jnp.bfloat16)
    return high, (values - high.astype(jnp.float32)).astype(jnp.bfloat16)


def mm(left, right):
    return dot(left[0], right[0]) + (dot(left[0], right[1]) + dot(left[1], right[0]))


def factor_chain(squares, key_grams, scales):
    size = squares[0].shape[0]
    row = lax.broadcasted_iota(jnp.int32, (size, size), 0)
    col = lax.broadcasted_iota(jnp.int32, (size, size), 1)
    eye = jnp.where(row == col, jnp.float32(linear_term), jnp.float32(0.0))
    inverses, powers = [], []
    for square, key_gram in zip(squares, key_grams):
        norm = jnp.maximum(jnp.sum(square * key_gram, keepdims=True), 0.0)
        inverses.append(lax.rsqrt(norm + 1e-06))
    key_splits = {id(g): split(g) for g in key_grams}
    for square, key_gram, inverse in zip(squares, key_grams, inverses):
        powers.append(mm(split(square * (inverse * inverse)), key_splits[id(key_gram)]))
    totals = None
    for step in range(NS_ITERS):
        parts = [split(p) for p in powers]
        squared = [mm(p, p) for p in parts]
        polys = [
            split(eye + cubic_term * p + quintic_term * s) for p, s in zip(powers, squared)
        ]
        if step < NS_ITERS - 1:
            once = [split(mm(q, p)) for q, p in zip(polys, parts)]
            powers = [mm(q, o) for q, o in zip(polys, once)]
        if totals is None:
            totals = polys
        elif step < NS_ITERS - 1:
            totals = [split(mm(q, t)) for q, t in zip(polys, totals)]
        else:
            totals = [mm(q, t) for q, t in zip(polys, totals)]
    return [t * (i * s) for t, i, s in zip(totals, inverses, scales)]


def owner_kernel(
    n, packed, weights, held, result,
    moved, mixed, lefts, rights, chain, total, send_sem, recv_sem, own_sem, weight_sem,
):
    local, width, hid = held.shape[0], held.shape[2], held.shape[3]
    tokens = n * moved.shape[3]
    me = lax.axis_index("ctx")

    loads = {}
    for l in range(local):
        for k in range(3):
            loads[l, k] = pltpu.make_async_copy(
                weights.at[l, k], held.at[l, k], weight_sem.at[l, k]
            )

    barrier = pltpu.get_barrier_semaphore()
    for j in range(1, n):
        pl.semaphore_signal(
            barrier, inc=1, device_id={"ctx": lax.rem(me + j, n)}, device_id_type=MESH
        )
    pl.semaphore_wait(barrier, n - 1)

    groups = (pl.ds(0, 2), pl.ds(2, 1))
    sends, owns = {}, {}
    for g in range(2):
        for l in range(local):
            owns[l, g] = pltpu.make_async_copy(
                packed.at[me, l, groups[g]], moved.at[me, l, groups[g]], own_sem.at[l, g]
            )
            owns[l, g].start()
            for j in range(1, n):
                target = lax.rem(me + j, n)
                sends[j, l, g] = pltpu.make_async_remote_copy(
                    src_ref=packed.at[target, l, groups[g]],
                    dst_ref=moved.at[me, l, groups[g]],
                    send_sem=send_sem.at[j - 1, l, g],
                    recv_sem=recv_sem.at[j - 1, l, g],
                    device_id={"ctx": target},
                    device_id_type=MESH,
                )
                sends[j, l, g].start()
    for l in range(local):
        for k in range(3):
            loads[l, k].start()

    def arrived(l, g):
        owns[l, g].wait()
        for j in range(1, n):
            sends[j, l, g].wait_recv()

    def rows(l, k):
        return moved[:, l, k].reshape(tokens, width)

    def columns(j):
        return pl.ds(pl.multiple_of(j * TILE, TILE), TILE)

    step_scale = math.sqrt(width / hid)
    for l in range(local):
        arrived(l, 0)
        for k in range(3):
            loads[l, k].wait()

        @pl.loop(0, hid // TILE)
        def _(j):
            cols = columns(j)
            keys, scaled = rows(l, 0), rows(l, 1)
            gate_pre = dot(keys, held[l, 0, :, cols].astype(jnp.bfloat16))
            up_proj = dot(keys, held[l, 1, :, cols].astype(jnp.bfloat16))
            back_grad = -dot(scaled, held[l, 2, :, cols].astype(jnp.bfloat16))
            sigmoid_gate = jax.nn.sigmoid(gate_pre)
            silu_gate = gate_pre * sigmoid_gate
            rights[l, 0, :, cols] = (
                back_grad * up_proj * sigmoid_gate * (1.0 + gate_pre * (1.0 - sigmoid_gate))
            ).astype(jnp.bfloat16)
            rights[l, 1, :, cols] = (back_grad * silu_gate).astype(jnp.bfloat16)
            rights[l, 2, :, cols] = (silu_gate * up_proj).astype(jnp.bfloat16)

        keys, scaled = rows(l, 0), rows(l, 1)
        lefts[l, 0] = keys.T
        lefts[l, 1] = scaled.T
        key_gram, scaled_gram = dot_rows(keys, keys), dot_rows(scaled, scaled)
        squares = [dot_rows(rights[l, k], rights[l, k]) for k in range(3)]
        factors = factor_chain(
            squares,
            [key_gram, key_gram, scaled_gram],
            [-step_scale, -step_scale, step_scale],
        )
        for k in range(3):
            chain[l, k] = factors[k].astype(jnp.bfloat16)

        @pl.loop(0, hid // TILE)
        def _(j):
            cols = columns(j)
            for k in range(3):
                mixed[l, k, :, cols] = dot(chain[l, k], rights[l, k, :, cols]).astype(
                    jnp.bfloat16
                )

    for l in range(local):
        arrived(l, 1)
        total[...] = jnp.zeros_like(total)

        @pl.loop(0, hid // TILE)
        def _(j):
            cols = columns(j)
            queries = rows(l, 2)
            applied = []
            for k in range(3):
                updated = held[l, k, :, cols] + dot(lefts[l, k // 2], mixed[l, k, :, cols])
                held[l, k, :, cols] = updated
                applied.append(updated.astype(jnp.bfloat16))
            gate_pre, up_proj = dot(queries, applied[0]), dot(queries, applied[1])
            hidden = (gate_pre * jax.nn.sigmoid(gate_pre) * up_proj).astype(jnp.bfloat16)
            total[...] += dot_rows(hidden, applied[2])

        result[:, l] = total[...].astype(jnp.bfloat16).reshape(result[:, l].shape)

    for copy in sends.values():
        copy.wait_send()


def owner_step(packed, fast_weights, n):
    local, _, width, hid = fast_weights.shape
    tokens = n * packed.shape[3]
    bf16, vmem = jnp.bfloat16, pl.BlockSpec(memory_space=pltpu.VMEM)
    return pl.pallas_call(
        functools.partial(owner_kernel, n),
        out_shape=(
            pltpu.VMEM(fast_weights.shape, jnp.float32),
            jax.ShapeDtypeStruct((n, local, packed.shape[3], width), bf16),
        ),
        in_specs=[pl.BlockSpec(memory_space=pl.ANY)] * 2,
        out_specs=(vmem, vmem),
        scratch_shapes=[
            pltpu.VMEM(packed.shape, bf16),
            pltpu.VMEM((local, 3, tokens, hid), bf16),
            pltpu.VMEM((local, 2, width, tokens), bf16),
            pltpu.VMEM((local, 3, tokens, hid), bf16),
            pltpu.VMEM((local, 3, tokens, tokens), bf16),
            pltpu.VMEM((tokens, width), jnp.float32),
            pltpu.SemaphoreType.DMA((n - 1, local, 2)),
            pltpu.SemaphoreType.DMA((n - 1, local, 2)),
            pltpu.SemaphoreType.DMA((local, 2)),
            pltpu.SemaphoreType.DMA((local, 3)),
        ],
        compiler_params=pltpu.CompilerParams(
            collective_id=0, has_side_effects=True, vmem_limit_bytes=24 * 2**20
        ),
    )(packed, fast_weights)


def store_kernel(held, out, sems):
    copies = [
        pltpu.make_async_copy(held.at[l, k], out.at[l, k], sems.at[l, k])
        for l in range(held.shape[0])
        for k in range(held.shape[1])
    ]
    for copy in copies:
        copy.start()
    for copy in copies:
        copy.wait()


def store(held):
    return pl.pallas_call(
        store_kernel,
        out_shape=jax.ShapeDtypeStruct(held.shape, held.dtype),
        in_specs=[pl.BlockSpec(memory_space=pltpu.VMEM)],
        out_specs=pl.BlockSpec(memory_space=pl.ANY),
        scratch_shapes=[pltpu.SemaphoreType.DMA(held.shape[:2])],
        compiler_params=pltpu.CompilerParams(vmem_limit_bytes=8 * 2**20),
        cost_estimate=pl.CostEstimate(
            flops=0, bytes_accessed=8 * held.size, transcendentals=0
        ),
    )(held)


def body(query_rows, key_rows, value_rows, token_rates, fast_weights):
    n = lax.axis_size("ctx")
    local = fast_weights.shape[0]
    tokens, heads, width = key_rows.shape
    scaled = (
        token_rates.astype(jnp.float32)[:, :, None] * value_rows.astype(jnp.float32)
    ).astype(jnp.bfloat16)
    packed = jnp.stack([key_rows, scaled, query_rows]).transpose(2, 0, 1, 3)
    packed = packed.reshape(n, local, 3, tokens, width)
    held, result = owner_step(packed, fast_weights, n)
    outputs = lax.all_to_all(
        result.reshape(heads, tokens, width), "ctx", split_axis=0, concat_axis=0, tiled=True
    )
    new_weights = store(held)
    return (outputs.transpose(1, 0, 2), new_weights)


def solution(mesh):
    placed = (
        P(("dp", "ctx"), None, None),
        P(("dp", "ctx"), None, None),
        P(("dp", "ctx"), None, None),
        P(("dp", "ctx"), None),
        P("ctx", None, None, None),
    )
    return jax.shard_map(
        body,
        mesh=mesh,
        in_specs=placed,
        out_specs=(P(("dp", "ctx"), None, None), P(("dp", "ctx"), None, None, None)),
        check_vma=False,
    )
```

```python
import functools
import math

import jax
import jax.numpy as jnp
from jax import lax
from jax.experimental import pallas as pl
from jax.experimental.pallas import tpu as pltpu
from jax.sharding import PartitionSpec as P

NS_ITERS = 3
TILE = 256
MESH = pl.DeviceIdType.MESH

linear_term = 3.4445
cubic_term = -4.775
quintic_term = 2.0315


def dot(left, right):
    return jnp.dot(left, right, preferred_element_type=jnp.float32)


def dot_rows(left, right):
    return lax.dot_general(
        left, right, (((1,), (1,)), ((), ())), preferred_element_type=jnp.float32
    )


def split(values):
    high = values.astype(jnp.bfloat16)
    return high, (values - high.astype(jnp.float32)).astype(jnp.bfloat16)


def mm(left, right):
    return dot(left[0], right[0]) + (dot(left[0], right[1]) + dot(left[1], right[0]))


def factor_chain(squares, key_grams, scales):
    size = squares[0].shape[0]
    row = lax.broadcasted_iota(jnp.int32, (size, size), 0)
    col = lax.broadcasted_iota(jnp.int32, (size, size), 1)
    eye = jnp.where(row == col, jnp.float32(linear_term), jnp.float32(0.0))
    inverses, powers = [], []
    for square, key_gram in zip(squares, key_grams):
        norm = jnp.maximum(jnp.sum(square * key_gram, keepdims=True), 0.0)
        inverses.append(lax.rsqrt(norm + 1e-06))
    key_splits = {id(g): split(g) for g in key_grams}
    for square, key_gram, inverse in zip(squares, key_grams, inverses):
        powers.append(mm(split(square * (inverse * inverse)), key_splits[id(key_gram)]))
    totals = None
    for step in range(NS_ITERS):
        parts = [split(p) for p in powers]
        squared = [mm(p, p) for p in parts]
        polys = [
            split(eye + cubic_term * p + quintic_term * s) for p, s in zip(powers, squared)
        ]
        if step < NS_ITERS - 1:
            once = [split(mm(q, p)) for q, p in zip(polys, parts)]
            powers = [mm(q, o) for q, o in zip(polys, once)]
        if totals is None:
            totals = polys
        elif step < NS_ITERS - 1:
            totals = [split(mm(q, t)) for q, t in zip(polys, totals)]
        else:
            totals = [mm(q, t) for q, t in zip(polys, totals)]
    return [t * (i * s) for t, i, s in zip(totals, inverses, scales)]


def owner_kernel(
    n, packed, weights, held, out,
    moved, mixed, lefts, rights, chain, total, result, landed,
    send_sem, recv_sem, own_sem, weight_sem, out_send_sem, out_recv_sem, out_own_sem,
):
    local, width, hid = held.shape[0], held.shape[2], held.shape[3]
    tokens = n * moved.shape[3]
    me = lax.axis_index("ctx")

    loads = {}
    for l in range(local):
        for k in range(3):
            loads[l, k] = pltpu.make_async_copy(
                weights.at[l, k], held.at[l, k], weight_sem.at[l, k]
            )

    barrier = pltpu.get_barrier_semaphore()
    for j in range(1, n):
        pl.semaphore_signal(
            barrier, inc=1, device_id={"ctx": lax.rem(me + j, n)}, device_id_type=MESH
        )
    pl.semaphore_wait(barrier, n - 1)

    groups = (pl.ds(0, 2), pl.ds(2, 1))
    sends, owns = {}, {}
    for g in range(2):
        for l in range(local):
            owns[l, g] = pltpu.make_async_copy(
                packed.at[me, l, groups[g]], moved.at[me, l, groups[g]], own_sem.at[l, g]
            )
            owns[l, g].start()
            for j in range(1, n):
                target = lax.rem(me + j, n)
                sends[j, l, g] = pltpu.make_async_remote_copy(
                    src_ref=packed.at[target, l, groups[g]],
                    dst_ref=moved.at[me, l, groups[g]],
                    send_sem=send_sem.at[j - 1, l, g],
                    recv_sem=recv_sem.at[j - 1, l, g],
                    device_id={"ctx": target},
                    device_id_type=MESH,
                )
                sends[j, l, g].start()
    for l in range(local):
        for k in range(3):
            loads[l, k].start()

    def arrived(l, g):
        owns[l, g].wait()
        for j in range(1, n):
            sends[j, l, g].wait_recv()

    def rows(l, k):
        return moved[:, l, k].reshape(tokens, width)

    def columns(j):
        return pl.ds(pl.multiple_of(j * TILE, TILE), TILE)

    step_scale = math.sqrt(width / hid)
    for l in range(local):
        arrived(l, 0)
        for k in range(3):
            loads[l, k].wait()

        @pl.loop(0, hid // TILE)
        def _(j):
            cols = columns(j)
            keys, scaled = rows(l, 0), rows(l, 1)
            gate_pre = dot(keys, held[l, 0, :, cols].astype(jnp.bfloat16))
            up_proj = dot(keys, held[l, 1, :, cols].astype(jnp.bfloat16))
            back_grad = -dot(scaled, held[l, 2, :, cols].astype(jnp.bfloat16))
            sigmoid_gate = jax.nn.sigmoid(gate_pre)
            silu_gate = gate_pre * sigmoid_gate
            rights[l, 0, :, cols] = (
                back_grad * up_proj * sigmoid_gate * (1.0 + gate_pre * (1.0 - sigmoid_gate))
            ).astype(jnp.bfloat16)
            rights[l, 1, :, cols] = (back_grad * silu_gate).astype(jnp.bfloat16)
            rights[l, 2, :, cols] = (silu_gate * up_proj).astype(jnp.bfloat16)

        keys, scaled = rows(l, 0), rows(l, 1)
        lefts[l, 0] = keys.T
        lefts[l, 1] = scaled.T
        key_gram, scaled_gram = dot_rows(keys, keys), dot_rows(scaled, scaled)
        squares = [dot_rows(rights[l, k], rights[l, k]) for k in range(3)]
        factors = factor_chain(
            squares,
            [key_gram, key_gram, scaled_gram],
            [-step_scale, -step_scale, step_scale],
        )
        for k in range(3):
            chain[l, k] = factors[k].astype(jnp.bfloat16)

        @pl.loop(0, hid // TILE)
        def _(j):
            cols = columns(j)
            for k in range(3):
                mixed[l, k, :, cols] = dot(chain[l, k], rights[l, k, :, cols]).astype(
                    jnp.bfloat16
                )

    returns = {}
    for l in range(local):
        arrived(l, 1)
        total[...] = jnp.zeros_like(total)

        @pl.loop(0, hid // TILE)
        def _(j):
            cols = columns(j)
            queries = rows(l, 2)
            applied = []
            for k in range(3):
                updated = held[l, k, :, cols] + dot(lefts[l, k // 2], mixed[l, k, :, cols])
                held[l, k, :, cols] = updated
                applied.append(updated.astype(jnp.bfloat16))
            gate_pre, up_proj = dot(queries, applied[0]), dot(queries, applied[1])
            hidden = (gate_pre * jax.nn.sigmoid(gate_pre) * up_proj).astype(jnp.bfloat16)
            total[...] += dot_rows(hidden, applied[2])

        result[:, l] = total[...].astype(jnp.bfloat16).reshape(n, tokens // n, width)
        returns[0, l] = pltpu.make_async_copy(
            result.at[me, l], landed.at[me, l], out_own_sem.at[l]
        )
        returns[0, l].start()
        for j in range(1, n):
            target = lax.rem(me + j, n)
            returns[j, l] = pltpu.make_async_remote_copy(
                src_ref=result.at[target, l],
                dst_ref=landed.at[me, l],
                send_sem=out_send_sem.at[j - 1, l],
                recv_sem=out_recv_sem.at[j - 1, l],
                device_id={"ctx": target},
                device_id_type=MESH,
            )
            returns[j, l].start()

    for copy in sends.values():
        copy.wait_send()
    for copy in returns.values():
        copy.wait()
    out[...] = landed[...]


def owner_step(packed, fast_weights, n):
    local, _, width, hid = fast_weights.shape
    tokens = n * packed.shape[3]
    bf16, vmem = jnp.bfloat16, pl.BlockSpec(memory_space=pltpu.VMEM)
    return pl.pallas_call(
        functools.partial(owner_kernel, n),
        out_shape=(
            pltpu.VMEM(fast_weights.shape, jnp.float32),
            jax.ShapeDtypeStruct((n, local, packed.shape[3], width), bf16),
        ),
        in_specs=[pl.BlockSpec(memory_space=pl.ANY)] * 2,
        out_specs=(vmem, vmem),
        scratch_shapes=[
            pltpu.VMEM(packed.shape, bf16),
            pltpu.VMEM((local, 3, tokens, hid), bf16),
            pltpu.VMEM((local, 2, width, tokens), bf16),
            pltpu.VMEM((local, 3, tokens, hid), bf16),
            pltpu.VMEM((local, 3, tokens, tokens), bf16),
            pltpu.VMEM((tokens, width), jnp.float32),
            pltpu.VMEM((n, local, packed.shape[3], width), bf16),
            pltpu.VMEM((n, local, packed.shape[3], width), bf16),
            pltpu.SemaphoreType.DMA((n - 1, local, 2)),
            pltpu.SemaphoreType.DMA((n - 1, local, 2)),
            pltpu.SemaphoreType.DMA((local, 2)),
            pltpu.SemaphoreType.DMA((local, 3)),
            pltpu.SemaphoreType.DMA((n - 1, local)),
            pltpu.SemaphoreType.DMA((n - 1, local)),
            pltpu.SemaphoreType.DMA((local,)),
        ],
        compiler_params=pltpu.CompilerParams(
            collective_id=0, has_side_effects=True, vmem_limit_bytes=24 * 2**20
        ),
    )(packed, fast_weights)


def store_kernel(held, out, sems):
    copies = [
        pltpu.make_async_copy(held.at[l, k], out.at[l, k], sems.at[l, k])
        for l in range(held.shape[0])
        for k in range(held.shape[1])
    ]
    for copy in copies:
        copy.start()
    for copy in copies:
        copy.wait()


def store(held):
    return pl.pallas_call(
        store_kernel,
        out_shape=jax.ShapeDtypeStruct(held.shape, held.dtype),
        in_specs=[pl.BlockSpec(memory_space=pltpu.VMEM)],
        out_specs=pl.BlockSpec(memory_space=pl.ANY),
        scratch_shapes=[pltpu.SemaphoreType.DMA(held.shape[:2])],
        compiler_params=pltpu.CompilerParams(vmem_limit_bytes=8 * 2**20),
        cost_estimate=pl.CostEstimate(
            flops=0, bytes_accessed=8 * held.size, transcendentals=0
        ),
    )(held)


def body(query_rows, key_rows, value_rows, token_rates, fast_weights):
    n = lax.axis_size("ctx")
    local = fast_weights.shape[0]
    tokens, heads, width = key_rows.shape
    scaled = (
        token_rates.astype(jnp.float32)[:, :, None] * value_rows.astype(jnp.float32)
    ).astype(jnp.bfloat16)
    packed = jnp.stack([key_rows, scaled, query_rows]).transpose(2, 0, 1, 3)
    packed = packed.reshape(n, local, 3, tokens, width)
    held, outputs = owner_step(packed, fast_weights, n)
    new_weights = store(held)
    outputs = outputs.reshape(heads, tokens, width)
    return (outputs.transpose(1, 0, 2), new_weights)


def solution(mesh):
    placed = (
        P(("dp", "ctx"), None, None),
        P(("dp", "ctx"), None, None),
        P(("dp", "ctx"), None, None),
        P(("dp", "ctx"), None),
        P("ctx", None, None, None),
    )
    return jax.shard_map(
        body,
        mesh=mesh,
        in_specs=placed,
        out_specs=(P(("dp", "ctx"), None, None), P(("dp", "ctx"), None, None, None)),
        check_vma=False,
    )
```
